32 devices in a mesh: blocks: 2 (over y), space: 4 (over z), view: 4 (over x, core).
Axes of the slice: x: 2, y: 2, z: 4, core: 2. Of those that a mesh axis runs over, the one named last changes fastest.
Arguments:
- estimate: float32 [64, 512, 128], P('space', 'blocks'), parts along dimension 1, may hold values from 0.5 to 7.5
- observed: float32 [4, 64, 512, 128], P('view', 'space', 'blocks'), parts along dimension 2, may hold values from 0.25 to 31.5
- valid: int32 [4, 64, 512, 128], P('view', 'space', 'blocks'), parts along dimension 2, may hold values 0 or 1
- psf_spectrum: float32 [4, 2, 64, 256, 128], P('view', None, None, 'space'), may hold values from -1 to 1, as said below
Outputs:
- refined: float32 [64, 512, 128], P('space', 'blocks'), parts along dimension 1
The draws below stay inside these ranges and needn't reach their ends.
There are 2 independent parts, one for each index of `blocks`. The reference program is written for one: setup_inputs(seed, part) draws one part's arguments, and reference() takes and returns one part's arrays. A program takes and returns all parts, laid end to end along the dimension named above; an argument that names none is the same for every part. Nothing has to cross between parts.
Inputs may be any that keep to these rules, and one draw needn't show every extreme that they name: `valid`: 1 marks a voxel that the view records, 0 one that it does not. `psf_spectrum`: for each view, the discrete Fourier transform, as in the reference program, of a point-spread function that is nonnegative at every voxel and sums to one.
All inputs are finite; a program needn't handle non-finite values. No bound on the sum of `valid` on one device may be relied on, other than what follows from the above.
Results may differ from the reference program's by a relative error of at most 0.00013.
Values sent between devices are 32-bit elements; how exact they have to be, the bound alone decides.
A program may use at most 128 MiB of HBM per device.

```python
import math
import jax
import jax.numpy as jnp
from jax import lax

NZ = 64
NX = 256
NY = 128
ITERS = 2
VIEWS = 4


HIGHEST = lax.Precision.HIGHEST


def signed_offset(length):
    indices = jnp.arange(length, dtype=jnp.int32)
    return ((indices + length // 2) % length - length // 2).astype(jnp.float32)


def dft_pair(length):
    indices = jnp.arange(length, dtype=jnp.int32)
    phases = indices[:, None] * indices[None, :] % length
    angles = phases.astype(jnp.float32) * (2.0 * math.pi / length)
    return (jnp.cos(angles), jnp.sin(angles))


def complex_forward(form, cosines, sines, real_part, imaginary):
    new_real = jnp.einsum(form, cosines, real_part, precision=HIGHEST) + jnp.einsum(form, sines, imaginary, precision=HIGHEST)
    new_imaginary = jnp.einsum(form, cosines, imaginary, precision=HIGHEST) - jnp.einsum(form, sines, real_part, precision=HIGHEST)
    return (new_real, new_imaginary)


def draw_estimate(key, part):
    base_key = jax.random.fold_in(key, 101)
    ground_key, spot_key, bright_key = jax.random.split(base_key, 3)
    shape = (NZ, NX, NY)
    ground = jax.random.uniform(ground_key, shape, jnp.float32, 0.5, 1.5)
    spots = jax.random.bernoulli(spot_key, 0.03, shape)
    bright = jax.random.uniform(bright_key, shape, jnp.float32, 2.0, 6.0)
    return ground + jnp.where(spots, bright, 0.0)


def draw_observed(key, part):
    base_key = jax.random.fold_in(key, 202)
    ground_key, spot_key, bright_key = jax.random.split(base_key, 3)
    shape = (VIEWS, NZ, NX, NY)
    ground = jax.random.uniform(ground_key, shape, jnp.float32, 0.5, 1.5)
    spots = jax.random.bernoulli(spot_key, 0.02, shape)
    bright = jax.random.uniform(bright_key, shape, jnp.float32, 10.0, 30.0)
    return ground + jnp.where(spots, bright, 0.0)


def draw_psf_spectrum(key, part):
    depth_off = signed_offset(NZ)[:, None, None]
    row_off = signed_offset(NX)[None, :, None]
    column_off = signed_offset(NY)[None, None, :]
    depth_cos, depth_sin = dft_pair(NZ)
    row_cos, row_sin = dft_pair(NX)
    column_cos, column_sin = dft_pair(NY)
    floor_share = 0.08
    voxel_total = NZ * NX * NY

    def one_view(view_key):
        width_key, rough_key = jax.random.split(view_key)
        picks = jax.random.uniform(width_key, (4,), jnp.float32)
        short_width = 0.8 + 0.5 * picks[0]
        side_width = 0.8 + 0.5 * picks[1]
        long_width = 8.0 + 8.0 * picks[2]
        rough = jax.random.uniform(rough_key, (NZ, NX, NY), jnp.float32, 0.5, 1.5)
        theta = 0.5 * math.pi * (picks[3] - 0.5)
        along = depth_off * jnp.cos(theta) + row_off * jnp.sin(theta)
        across = row_off * jnp.cos(theta) - depth_off * jnp.sin(theta)
        along_term = along / long_width
        across_term = across / short_width
        side_term = column_off / side_width
        quad = along_term * along_term + across_term * across_term + side_term * side_term
        kernel = jnp.exp(-0.5 * quad) * rough
        kernel = (1.0 - floor_share) * kernel / jnp.sum(kernel) + floor_share / voxel_total
        real_part = jnp.einsum('kx,zxy->zky', row_cos, kernel, precision=HIGHEST)
        imaginary = -jnp.einsum('kx,zxy->zky', row_sin, kernel, precision=HIGHEST)
        real_part, imaginary = complex_forward('ky,zxy->zxk', column_cos, column_sin, real_part, imaginary)
        real_part, imaginary = complex_forward('kz,zxy->kxy', depth_cos, depth_sin, real_part, imaginary)
        return jnp.stack((real_part, imaginary))
    return lax.map(one_view, jax.random.split(key, VIEWS))


def touch_ends(result, key, smallest, high):
    place = [jax.random.randint(jax.random.fold_in(key, axis), (), 0, length) for axis, length in enumerate(result.shape)]
    widest = result.shape.index(max(result.shape))
    beside = place[:widest] + [(place[widest] + 1) % result.shape[widest]] + place[widest + 1:]
    return result.at[tuple(place)].set(smallest).at[tuple(beside)].set(high)


def setup_inputs(seed: int = 0, part: int = 0) -> dict:
    streams_of = jax.random.split(jax.random.key(seed), 5)
    part_keys = jax.random.split(jax.random.fold_in(streams_of[4], part), 5)
    return {
        "estimate": draw_estimate(jax.random.fold_in(jax.random.fold_in(streams_of[4], part), 71), part),
        "observed": draw_observed(jax.random.fold_in(jax.random.fold_in(streams_of[4], part), 71), part),
        "valid": touch_ends((jax.random.randint(part_keys[2], (VIEWS, NZ, NX, NY), 0, 4) < 3).astype(jnp.int32), jax.random.fold_in(part_keys[2], 1), 0, 1),
        "psf_spectrum": draw_psf_spectrum(jax.random.fold_in(streams_of[4], 71), part),
    }


def reference(estimate, observed, valid, psf_spectrum):
    view_count = observed.shape[0]
    for iteration in range(ITERS):
        spectrum = jnp.fft.fftn(estimate)

        def one_view(accumulated, items):
            observed_view, valid_view, kernel = items
            transfer = lax.complex(kernel[0], kernel[1])
            blurred = jnp.real(jnp.fft.ifftn(spectrum * transfer))
            valid_mask = valid_view.astype(jnp.float32)
            ratios = valid_mask * observed_view / blurred + (1.0 - valid_mask)
            correction = jnp.real(jnp.fft.ifftn(jnp.fft.fftn(ratios) * jnp.conj(transfer)))
            return accumulated + correction, None

        combined, unused = lax.scan(one_view, jnp.zeros_like(estimate), (observed, valid, psf_spectrum))
        estimate = estimate * combined / view_count
    return estimate
```

```python
import numpy as np

import jax
import jax.numpy as jnp
from jax import lax
from jax.sharding import PartitionSpec as P

ITERS = 2

HIGH = lax.Precision.HIGH


def angles_of(rows, columns, length):
    return 2.0 * np.pi * (np.outer(rows, columns) % length) / length


class Tables:
    def __init__(self, depth, rows, columns, space):
        half = columns // 2
        local = rows // space
        y = np.arange(columns)
        k = np.arange(half)
        ang = angles_of(y, k, columns)
        self.half = half
        real, imag = np.cos(ang), -np.sin(ang)
        self.col_fwd = np.concatenate([real, imag], 1)
        self.col_fwd_turned = np.concatenate([imag, -real], 1)
        weight = np.where(k == 0, 1.0, 2.0)[:, None]
        norm = 1.0 / (depth * rows * columns)
        back_real, back_imag = weight * np.cos(ang.T) * norm, -weight * np.sin(ang.T) * norm
        self.col_inv = np.concatenate([back_real, back_imag], 0)
        self.col_inv_turned = np.concatenate([-back_imag, back_real], 0)
        self.alternate = np.where(y % 2 == 0, 1.0, -1.0)
        self.norm = norm
        x = np.arange(rows)
        ang = angles_of(x, x, rows)
        self.row_cos, self.row_sin = np.cos(ang), np.sin(ang)
        edge = np.zeros((rows, space, columns))
        edge_inv = np.zeros((space, columns, rows))
        for s in range(space):
            ang = angles_of(x, np.arange(local) + s * local, rows)
            edge[:, s, :local] = np.cos(ang)
            edge[:, s, half : half + local] = -np.sin(ang)
            edge_inv[s, :local] = np.cos(ang.T) * norm
            edge_inv[s, half : half + local] = -np.sin(ang.T) * norm
        self.edge, self.edge_inv = edge, edge_inv
        z = np.arange(depth)
        ang = angles_of(z, z, depth)
        self.depth_cos, self.depth_sin = np.cos(ang), np.sin(ang)


def f32(table):
    return jnp.asarray(table, jnp.float32)


def dot(form, *operands):
    return jnp.einsum(form, *operands, precision=HIGH, preferred_element_type=jnp.float32)


def turned(lanes):
    half = lanes.shape[-1] // 2
    return jnp.concatenate([lanes[..., half:], -lanes[..., :half]], -1)


def slab_forward(t, space, volume):
    planes, rows, columns = volume.shape
    one = dot("zxy,yl->zxl", volume, f32(t.col_fwd))
    two = dot("zxy,yl->zxl", volume, f32(t.col_fwd_turned))
    main = dot("kx,zxl->kzl", f32(t.row_cos), one) + dot("kx,zxl->kzl", f32(t.row_sin), two)
    last = jnp.sum(volume * f32(t.alternate), -1)
    edge = dot("zx,xsl->szl", last, f32(t.edge))
    main = main.reshape(space, rows // space, planes, columns)
    return jnp.concatenate([main, edge[:, None]], 1)


def slab_inverse(t, spectrum):
    space, local, planes, columns = spectrum.shape
    main = spectrum[:, :-1].reshape(space * (local - 1), planes, columns)
    edge = spectrum[:, -1]
    one = dot("xk,kzl->zxl", f32(t.row_cos), main)
    two = dot("xk,kzl->zxl", f32(t.row_sin), main)
    last = dot("szl,slx->zx", edge, f32(t.edge_inv))
    return (
        dot("zxl,ly->zxy", one, f32(t.col_inv))
        - dot("zxl,ly->zxy", two, f32(t.col_inv_turned))
        + last[:, :, None] * f32(t.alternate)
    )


def depth_forward(t, lanes):
    return dot("kz,rzl->rkl", f32(t.depth_cos), lanes) + dot("kz,rzl->rkl", f32(t.depth_sin), turned(lanes))


def depth_inverse(t, lanes):
    return dot("zk,rkl->rzl", f32(t.depth_cos), lanes) - dot("zk,rkl->rzl", f32(t.depth_sin), turned(lanes))


def filtered(lanes, real, imag, sign):
    return lanes * real - sign * turned(lanes) * imag


def shards(estimate, observed, valid, psf_spectrum):
    space = lax.axis_size("space")
    views = lax.axis_size("view")
    planes, rows, columns = estimate.shape
    depth = planes * space
    local = rows // space
    half = columns // 2
    t = Tables(depth, rows, columns, space)
    view_count = observed.shape[0] * views
    shared = planes % views == 0
    share = planes // views if shared else planes

    psf = jnp.swapaxes(psf_spectrum[0], 1, 2)
    last = jnp.pad(jnp.swapaxes(psf[..., half], 1, 2), ((0, 0), (0, 0), (0, half - local)))
    psf = jnp.concatenate([psf[..., :half], last[:, None]], 1)
    psf = jnp.concatenate([psf, psf], -1)
    psf_real, psf_imag = psf[0], psf[1]

    def to_pencil(spectrum):
        parts = lax.all_to_all(spectrum, "space", 0, 0)
        return jnp.swapaxes(parts, 0, 1).reshape(local + 1, depth, columns)

    def to_slab(pencil):
        parts = jnp.swapaxes(pencil.reshape(local + 1, space, planes, columns), 0, 1)
        return lax.all_to_all(parts, "space", 0, 0)

    if shared:
        estimate = lax.dynamic_slice_in_dim(estimate, lax.axis_index("view") * share, share, 0)
    observed, valid = observed[0], valid[0].astype(jnp.float32)
    masked = valid * observed

    for iteration in range(ITERS):
        parts = lax.all_to_all(slab_forward(t, space, estimate), "space", 0, 0)
        if shared:
            parts = lax.all_gather(parts, "view")
            pencil = parts.transpose(2, 1, 0, 3, 4).reshape(local + 1, depth, columns)
        else:
            pencil = jnp.swapaxes(parts, 0, 1).reshape(local + 1, depth, columns)
        blurred = depth_inverse(t, filtered(depth_forward(t, pencil), psf_real, psf_imag, 1.0))
        ratio = masked / slab_inverse(t, to_slab(blurred)) + (1.0 - valid)
        pencil = to_pencil(slab_forward(t, space, ratio))
        correction = depth_inverse(t, filtered(depth_forward(t, pencil), psf_real, psf_imag, -1.0))
        if shared:
            correction = correction.reshape(local + 1, space, views, share, columns).transpose(2, 1, 0, 3, 4)
            correction = lax.psum_scatter(correction, "view", scatter_dimension=0)
            correction = lax.all_to_all(correction, "space", 0, 0)
        else:
            correction = to_slab(lax.psum(correction, "view"))
        estimate = estimate * slab_inverse(t, correction) / view_count
    if shared:
        estimate = lax.all_gather(estimate, "view", axis=0, tiled=True)
    return estimate


def solution(mesh):
    return jax.shard_map(
        shards,
        mesh=mesh,
        in_specs=(
            P("space", "blocks", None),
            P("view", "space", "blocks", None),
            P("view", "space", "blocks", None),
            P("view", None, None, "space", None),
        ),
        out_specs=P("space", "blocks", None),
        check_vma=False,
    )
```

```python
import functools

import numpy as np

import jax
import jax.numpy as jnp
from jax import lax
from jax.experimental import pallas as pl
from jax.experimental.pallas import tpu as pltpu
from jax.sharding import PartitionSpec as P

ITERS = 2

HIGH = lax.Precision.HIGH


def angles_of(rows, columns, length):
    return 2.0 * np.pi * (np.outer(rows, columns) % length) / length


class Tables:
    def __init__(self, depth, rows, columns, space):
        half = columns // 2
        local = rows // space
        y = np.arange(columns)
        k = np.arange(half)
        ang = angles_of(y, k, columns)
        self.half = half
        real, imag = np.cos(ang), -np.sin(ang)
        self.col_fwd = np.concatenate([real, imag], 1)
        self.col_fwd_turned = np.concatenate([imag, -real], 1)
        weight = np.where(k == 0, 1.0, 2.0)[:, None]
        norm = 1.0 / (depth * rows * columns)
        back_real, back_imag = weight * np.cos(ang.T) * norm, -weight * np.sin(ang.T) * norm
        self.col_inv = np.concatenate([back_real, back_imag], 0)
        self.col_inv_turned = np.concatenate([-back_imag, back_real], 0)
        self.alternate = np.where(y % 2 == 0, 1.0, -1.0)
        self.norm = norm
        x = np.arange(rows)
        ang = angles_of(x, x, rows)
        self.row_cos, self.row_sin = np.cos(ang), np.sin(ang)
        edge = np.zeros((rows, space, columns))
        edge_inv = np.zeros((space, columns, rows))
        for s in range(space):
            ang = angles_of(x, np.arange(local) + s * local, rows)
            edge[:, s, :local] = np.cos(ang)
            edge[:, s, half : half + local] = -np.sin(ang)
            edge_inv[s, :local] = np.cos(ang.T) * norm
            edge_inv[s, half : half + local] = -np.sin(ang.T) * norm
        self.edge, self.edge_inv = edge, edge_inv
        z = np.arange(depth)
        ang = angles_of(z, z, depth)
        self.depth_cos, self.depth_sin = np.cos(ang), np.sin(ang)


def f32(table):
    return jnp.asarray(table, jnp.float32)


def dot(form, *operands):
    return jnp.einsum(form, *operands, precision=HIGH, preferred_element_type=jnp.float32)


def turned(lanes):
    half = lanes.shape[-1] // 2
    return jnp.concatenate([lanes[..., half:], -lanes[..., :half]], -1)


def slab_forward(t, space, volume):
    planes, rows, columns = volume.shape
    one = dot("zxy,yl->zxl", volume, f32(t.col_fwd))
    two = dot("zxy,yl->zxl", volume, f32(t.col_fwd_turned))
    main = dot("kx,zxl->kzl", f32(t.row_cos), one) + dot("kx,zxl->kzl", f32(t.row_sin), two)
    last = jnp.sum(volume * f32(t.alternate), -1)
    edge = dot("zx,xsl->szl", last, f32(t.edge))
    main = main.reshape(space, rows // space, planes, columns)
    return jnp.concatenate([main, edge[:, None]], 1)


def slab_inverse(t, spectrum):
    space, local, planes, columns = spectrum.shape
    main = spectrum[:, :-1].reshape(space * (local - 1), planes, columns)
    edge = spectrum[:, -1]
    one = dot("xk,kzl->zxl", f32(t.row_cos), main)
    two = dot("xk,kzl->zxl", f32(t.row_sin), main)
    last = dot("szl,slx->zx", edge, f32(t.edge_inv))
    return (
        dot("zxl,ly->zxy", one, f32(t.col_inv))
        - dot("zxl,ly->zxy", two, f32(t.col_inv_turned))
        + last[:, :, None] * f32(t.alternate)
    )


def depth_forward(t, lanes):
    return dot("kz,rzl->rkl", f32(t.depth_cos), lanes) + dot("kz,rzl->rkl", f32(t.depth_sin), turned(lanes))


def depth_inverse(t, lanes):
    return dot("zk,rkl->rzl", f32(t.depth_cos), lanes) - dot("zk,rkl->rzl", f32(t.depth_sin), turned(lanes))


def filtered(lanes, real, imag, sign):
    return lanes * real - sign * turned(lanes) * imag


def shards(estimate, observed, valid, psf_spectrum):
    space = lax.axis_size("space")
    views = lax.axis_size("view")
    planes, rows, columns = estimate.shape
    depth = planes * space
    local = rows // space
    half = columns // 2
    t = Tables(depth, rows, columns, space)
    view_count = observed.shape[0] * views
    shared = planes % views == 0
    share = planes // views if shared else planes

    psf = jnp.swapaxes(psf_spectrum[0], 1, 2)
    last = jnp.pad(jnp.swapaxes(psf[..., half], 1, 2), ((0, 0), (0, 0), (0, half - local)))
    psf = jnp.concatenate([psf[..., :half], last[:, None]], 1)
    psf = jnp.concatenate([psf, psf], -1)
    psf_real, psf_imag = psf[0], psf[1]

    def to_pencil(spectrum):
        parts = lax.all_to_all(spectrum, "space", 0, 0)
        return jnp.swapaxes(parts, 0, 1).reshape(local + 1, depth, columns)

    def to_slab(pencil):
        parts = jnp.swapaxes(pencil.reshape(local + 1, space, planes, columns), 0, 1)
        return lax.all_to_all(parts, "space", 0, 0)

    if shared:
        estimate = lax.dynamic_slice_in_dim(estimate, lax.axis_index("view") * share, share, 0)
    observed, valid = observed[0], valid[0].astype(jnp.float32)
    masked = valid * observed

    for iteration in range(ITERS):
        parts = lax.all_to_all(slab_forward(t, space, estimate), "space", 0, 0)
        if shared:
            parts = lax.all_gather(parts, "view")
            pencil = parts.transpose(2, 1, 0, 3, 4).reshape(local + 1, depth, columns)
        else:
            pencil = jnp.swapaxes(parts, 0, 1).reshape(local + 1, depth, columns)
        blurred = depth_inverse(t, filtered(depth_forward(t, pencil), psf_real, psf_imag, 1.0))
        ratio = masked / slab_inverse(t, to_slab(blurred)) + (1.0 - valid)
        pencil = to_pencil(slab_forward(t, space, ratio))
        correction = depth_inverse(t, filtered(depth_forward(t, pencil), psf_real, psf_imag, -1.0))
        if shared:
            correction = correction.reshape(local + 1, space, views, share, columns).transpose(2, 1, 0, 3, 4)
            correction = lax.psum_scatter(correction, "view", scatter_dimension=0)
            correction = lax.all_to_all(correction, "space", 0, 0)
        else:
            correction = to_slab(lax.psum(correction, "view"))
        estimate = estimate * slab_inverse(t, correction) / view_count
    if shared:
        estimate = lax.all_gather(estimate, "view", axis=0, tiled=True)
    return estimate


def split(value):
    high = value.astype(jnp.bfloat16)
    return high, (value - high.astype(jnp.float32)).astype(jnp.bfloat16)


def table_pair(table):
    high = np.asarray(table, np.float32).astype(jnp.bfloat16)
    low = (np.asarray(table, np.float32) - high.astype(np.float32)).astype(jnp.bfloat16)
    return jnp.asarray(np.stack([high, low]))


def product(left, right):
    form = functools.partial(jnp.dot, preferred_element_type=jnp.float32)
    return form(left[0], right[0]) + form(left[0], right[1]) + form(left[1], right[0])


def across(left, right):
    return lax.dot_general(
        left,
        right,
        (((1,), (1,)), ((), ())),
        precision=lax.Precision.HIGHEST,
        preferred_element_type=jnp.float32,
    )


def iteration_kernel(
    sizes, est, observed, valid, psf, psf_last, col_fwd, col_inv, row_fwd, row_inv, edge, edge_back,
    dep_fwd, dep_inv, dep_last_fwd, dep_last_inv, out,
    a_send, a_recv, b_send, b_recv, c_send, c_recv, d_send, d_recv, e_send, e_recv,
    a_sems, g_sems, b_sems, c_sems, d_sems, e_sems,
):
    space, views, planes, share, rows, columns, depth = sizes
    local = rows // space
    half = columns // 2
    block = share * local + 8
    me = lax.axis_index("space")
    view = lax.axis_index("view")
    hops = []
    hop = views // 2
    while hop:
        hops.append(hop)
        hop //= 2

    def partner(hop, index):
        return index + hop - 2 * hop * ((index // hop) % 2)

    def peer(step):
        return lax.rem(me + step, space)

    def part(index, count=1):
        return pl.ds(pl.multiple_of(index * block, 8), count * block)

    barrier = pltpu.get_barrier_semaphore()
    for step in range(1, space):
        pl.semaphore_signal(barrier, inc=1, device_id={"space": peer(step)}, device_id_type=pl.DeviceIdType.MESH)
    for hop in hops:
        pl.semaphore_signal(barrier, inc=1, device_id={"view": partner(hop, view)}, device_id_type=pl.DeviceIdType.MESH)

    lane = lax.broadcasted_iota(jnp.int32, (8, columns), 1)
    line = lax.broadcasted_iota(jnp.int32, (8, columns), 0)
    alternate = jnp.where(lane % 2 == 0, 1.0, -1.0).astype(jnp.float32)
    sign = jnp.where(lane[:1] < half, 1.0, -1.0).astype(jnp.float32)

    def turn(value):
        return pltpu.roll(value, half, 1) * sign

    def alternate_of(plane):
        return jnp.where(line == plane, alternate, 0.0)

    def forward_plane(volume, store, plane, base, chunks):
        one = product(split(volume), (col_fwd[0], col_fwd[1]))
        both = jnp.concatenate([one[:, :columns], one[:, columns:]], 0)
        main = product((row_fwd[0], row_fwd[1]), split(both))
        for j in range(space):
            start = pl.multiple_of((j * chunks + base) * block + plane * local, 8)
            store[pl.ds(start, local), :] = main[j * local : (j + 1) * local]
        return across(alternate_of(plane), volume)

    def forward_last(sums, store, base, chunks):
        last = jnp.dot(sums, edge[...], precision=lax.Precision.HIGHEST, preferred_element_type=jnp.float32)
        for j in range(space):
            start = pl.multiple_of((j * chunks + base) * block + share * local, 8)
            store[pl.ds(start, 8), :] = last[:, j * columns : (j + 1) * columns]

    def inverse_last(held, base, chunks):
        last = jnp.concatenate(
            [held[pl.ds(pl.multiple_of((j * chunks + base) * block + share * local, 8), 8), :] for j in range(space)], 1
        )
        return across(edge_back[...], last)

    def inverse_plane(held, last, plane, base, chunks):
        main = jnp.concatenate(
            [
                held[pl.ds(pl.multiple_of((j * chunks + base) * block + plane * local, 8), local), :]
                for j in range(space)
            ],
            0,
        )
        both = product((row_inv[0], row_inv[1]), split(main))
        both = jnp.concatenate([both[:rows], both[rows:]], 1)
        value = product(split(both), (col_inv[0], col_inv[1]))
        return value + jnp.dot(
            last, alternate_of(plane), precision=lax.Precision.HIGHEST, preferred_element_type=jnp.float32
        )

    def filtered_pencil(held, store, conjugate):
        count = space * views
        left = lax.broadcasted_iota(jnp.int32, (1, columns), 1) < half

        def middle(value, real, imag):
            return value * real - (conjugate * turn(value)) * imag

        def doubled(start):
            value = psf[pl.ds(start, depth, stride=local), :]
            return jnp.where(left, value, pltpu.roll(value, half, 1))

        def group(g, carry):
            pieces = []
            for i in range(8):
                row = g * 8 + i
                pieces.append(
                    jnp.concatenate(
                        [held[pl.ds(p * local + row, count, stride=block), :] for p in range(share)], 0
                    )
                )
            wide = jnp.concatenate(
                [jnp.concatenate(pieces, 1), jnp.concatenate([turn(piece) for piece in pieces], 1)], 0
            )
            wide = product((dep_fwd[0], dep_fwd[1]), split(wide))
            pieces = []
            for i in range(8):
                row = g * 8 + i
                pieces.append(
                    middle(
                        wide[:, i * columns : (i + 1) * columns],
                        doubled(row),
                        doubled(depth * local + row),
                    )
                )
            wide = jnp.concatenate(
                [jnp.concatenate(pieces, 1), jnp.concatenate([turn(piece) for piece in pieces], 1)], 0
            )
            wide = product((dep_inv[0], dep_inv[1]), split(wide))
            for i in range(8):
                row = g * 8 + i
                for p in range(share):
                    value = wide[p * count : (p + 1) * count, i * columns : (i + 1) * columns]
                    store[pl.ds(p * local + row, count, stride=block), :] = value
            return carry

        lax.fori_loop(0, local // 8, group, 0)
        last = jnp.concatenate(
            [held[q * block + share * local : q * block + share * local + 8, :] for q in range(count)], 0
        )
        last = jnp.concatenate([last, turn(last)], 0)
        last = jnp.dot(
            dep_last_fwd[...], last, precision=lax.Precision.HIGHEST, preferred_element_type=jnp.float32
        )
        last = middle(last, psf_last[0], psf_last[1])
        last = jnp.concatenate([last, turn(last)], 0)
        last = jnp.dot(
            dep_last_inv[...], last, precision=lax.Precision.HIGHEST, preferred_element_type=jnp.float32
        )
        for q in range(count):
            store[q * block + share * local : q * block + share * local + 8, :] = last[q * 8 : (q + 1) * 8]

    def remote(source, target, sems, index, **device):
        return pltpu.make_async_remote_copy(
            src_ref=source,
            dst_ref=target,
            send_sem=sems.at[(0,) + index],
            recv_sem=sems.at[(1,) + index],
            device_id=device,
            device_id_type=pl.DeviceIdType.MESH,
        )

    def estimate_plane(plane, sums):
        return sums + forward_plane(est[plane], a_send, plane, 0, 1)

    sums = lax.fori_loop(0, share, estimate_plane, jnp.zeros((8, rows), jnp.float32))
    forward_last(sums, a_send, 0, 1)
    pl.semaphore_wait(barrier, space - 1 + len(hops))
    spread = []
    for step in range(1, space):
        j = peer(step)
        copy = remote(a_send.at[part(j)], a_recv.at[part(me * views + view)], a_sems, (step,), space=j)
        copy.start()
        spread.append(copy)
    a_recv[part(me * views + view), :] = a_send[part(me), :]
    held = [0]
    for level, hop in enumerate(hops):
        arrived = []
        for step in range(space):
            source = lax.rem(me - step + space, space)
            if level == 0 and step:
                spread[step - 1].wait()
            for order, offset in enumerate(held):
                owner = view
                for other in hops:
                    if offset & other:
                        owner = partner(other, owner)
                where = part(source * views + owner)
                copy = remote(
                    a_recv.at[where], a_recv.at[where], g_sems, (level, step, order), view=partner(hop, view)
                )
                copy.start()
                arrived.append(copy)
        for copy in arrived:
            copy.wait()
        held = held + [offset | hop for offset in held]

    filtered_pencil(a_recv, b_send, 1.0)

    sent = []
    for chunk in range(views):
        for step in range(1, space):
            j = peer(step)
            copy = remote(
                b_send.at[part(j * views + chunk)], b_recv.at[part(me * views + chunk)], b_sems, (chunk, step), space=j
            )
            copy.start()
            sent.append(copy)
    ratios = []
    for chunk in range(views):
        b_recv[part(me * views + chunk), :] = b_send[part(me * views + chunk), :]
        for step in range(1, space):
            sent[chunk * (space - 1) + step - 1].wait()
        last = inverse_last(b_recv, chunk, views)

        def ratio_plane(plane, sums, chunk=chunk, last=last):
            blurred = inverse_plane(b_recv, last, plane, chunk, views)
            mask = valid[chunk * share + plane].astype(jnp.float32)
            ratio = mask * observed[chunk * share + plane] / blurred + (1.0 - mask)
            return sums + forward_plane(ratio, c_send, plane, chunk, views)

        sums = lax.fori_loop(0, share, ratio_plane, jnp.zeros((8, rows), jnp.float32))
        forward_last(sums, c_send, chunk, views)
        c_recv[part(me * views + chunk), :] = c_send[part(me * views + chunk), :]
        for step in range(1, space):
            j = peer(step)
            copy = remote(
                c_send.at[part(j * views + chunk)], c_recv.at[part(me * views + chunk)], c_sems, (chunk, step), space=j
            )
            copy.start()
            ratios.append(copy)
    for copy in ratios:
        copy.wait()

    filtered_pencil(c_recv, d_send, -1.0)

    kept = [0]
    for hop in hops:
        kept = kept + [offset | hop for offset in kept]

    def chunk_of(offset):
        owner = view
        for other in hops:
            if offset & other:
                owner = partner(other, owner)
        return owner

    for level, hop in enumerate(reversed(hops)):
        copies = []
        keep = [offset for offset in kept if not offset & hop]
        for order, offset in enumerate(keep):
            for j in range(space):
                place = part(j * views + chunk_of(offset | hop))
                copy = remote(
                    d_send.at[place],
                    d_recv.at[part((level * views + order) * space + j)],
                    d_sems,
                    (level, order, j),
                    view=partner(hop, view),
                )
                copy.start()
                copies.append(copy)
        for order, offset in enumerate(keep):
            for j in range(space):
                copies[order * space + j].wait()
                place = part(j * views + chunk_of(offset))
                extra = d_recv[part((level * views + order) * space + j), :]
                if hop == hops[0]:
                    e_send[part(j), :] = d_send[place, :] + extra
                else:
                    d_send[place, :] = d_send[place, :] + extra
        kept = keep

    copies = []
    for step in range(1, space):
        j = peer(step)
        copy = remote(e_send.at[part(j)], e_recv.at[part(me)], e_sems, (step,), space=j)
        copy.start()
        copies.append(copy)
    e_recv[part(me), :] = e_send[part(me), :]
    for copy in copies:
        copy.wait()
    last = inverse_last(e_recv, 0, 1)

    def update_plane(plane, carry):
        out[plane] = est[plane] * inverse_plane(e_recv, last, plane, 0, 1) * (1.0 / views)
        return carry

    lax.fori_loop(0, share, update_plane, 0)


def kernel_tables(t, space, views, share):
    planes = share * views
    depth = planes * space
    s, c, p = np.meshgrid(np.arange(space), np.arange(views), np.arange(share), indexing="ij")
    z = (s * planes + c * share + p).transpose(2, 0, 1).reshape(-1)
    forward = np.concatenate([t.depth_cos[:, z], t.depth_sin[:, z]], 1)
    inverse = np.concatenate([t.depth_cos[z], -t.depth_sin[z]], 1)
    place = (np.arange(space * views)[:, None] * 8 + np.arange(share)[None, :]).reshape(-1)
    last_cos = np.zeros((depth, space * views * 8))
    last_sin = np.zeros((depth, space * views * 8))
    last_cos[:, place] = t.depth_cos
    last_sin[:, place] = t.depth_sin
    return (
        table_pair(np.concatenate([t.col_fwd, t.col_fwd_turned], 1)),
        table_pair(np.concatenate([t.col_inv, -t.col_inv_turned], 0)),
        table_pair(np.concatenate([t.row_cos, t.row_sin], 1)),
        table_pair(np.concatenate([t.row_cos, t.row_sin], 0)),
        f32(t.edge.reshape(t.edge.shape[0], -1)),
        f32(t.edge_inv.transpose(2, 0, 1).reshape(t.edge.shape[0], -1)),
        table_pair(forward),
        table_pair(inverse),
        f32(np.concatenate([last_cos, last_sin], 1)),
        f32(np.concatenate([last_cos.T, -last_sin.T], 1)),
    )


def kernel_shards(estimate, observed, valid, psf_spectrum):
    space = lax.axis_size("space")
    views = lax.axis_size("view")
    planes, rows, columns = estimate.shape
    depth = planes * space
    local = rows // space
    half = columns // 2
    share = planes // views
    block = share * local + 8
    t = Tables(depth, rows, columns, space)
    tables = kernel_tables(t, space, views, share)
    last = psf_spectrum[0, :, :, :, half]
    last = jnp.pad(last, ((0, 0), (0, 0), (0, half - local)))
    last = jnp.concatenate([last, last], -1)
    psf = psf_spectrum.reshape(2 * depth * local, columns)
    estimate = lax.dynamic_slice_in_dim(estimate, lax.axis_index("view") * share, share, 0)
    levels = max(views.bit_length() - 1, 1)
    big = pltpu.VMEM((space * views * block, columns), jnp.float32)
    small = pltpu.VMEM((space * block, columns), jnp.float32)
    operands = (observed[0], valid[0], psf, last) + tables
    call = pl.pallas_call(
        functools.partial(iteration_kernel, (space, views, planes, share, rows, columns, depth)),
        out_shape=jax.ShapeDtypeStruct(estimate.shape, jnp.float32),
        in_specs=[pl.BlockSpec(memory_space=pltpu.VMEM)] * (len(operands) + 1),
        out_specs=pl.BlockSpec(memory_space=pltpu.VMEM),
        scratch_shapes=[
            small, big, big, big, big, big, big,
            pltpu.VMEM((levels * views * space * block, columns), jnp.float32),
            small, small,
            pltpu.SemaphoreType.DMA((2, space)),
            pltpu.SemaphoreType.DMA((2, levels, space, views)),
            pltpu.SemaphoreType.DMA((2, views, space)),
            pltpu.SemaphoreType.DMA((2, views, space)),
            pltpu.SemaphoreType.DMA((2, levels, views, space)),
            pltpu.SemaphoreType.DMA((2, space)),
        ],
        compiler_params=pltpu.CompilerParams(
            collective_id=0, has_side_effects=True, vmem_limit_bytes=56 * 1024 * 1024
        ),
        name="iteration",
    )
    for iteration in range(ITERS):
        estimate = call(estimate, *operands)
    return lax.all_gather(estimate, "view", axis=0, tiled=True)


def fits(mesh, estimate, observed):
    space, views = mesh.shape["space"], mesh.shape["view"]
    planes = estimate.shape[0] // space
    local = observed.shape[2] // mesh.shape["blocks"] // space
    return (
        planes % views == 0
        and planes // views <= 8
        and local % 8 == 0
        and views > 1
        and views & (views - 1) == 0
        and observed.shape[0] == views
    )


def solution(mesh):
    def mapped(body):
        return jax.shard_map(
            body,
            mesh=mesh,
            in_specs=(
                P("space", "blocks", None),
                P("view", "space", "blocks", None),
                P("view", "space", "blocks", None),
                P("view", None, None, "space", None),
            ),
            out_specs=P("space", "blocks", None),
            check_vma=False,
        )

    def refine(estimate, observed, valid, psf_spectrum):
        body = kernel_shards if fits(mesh, estimate, observed) else shards
        return mapped(body)(estimate, observed, valid, psf_spectrum)

    return refine
```

```python
import functools

import numpy as np

import jax
import jax.numpy as jnp
from jax import lax
from jax.experimental import pallas as pl
from jax.experimental.pallas import tpu as pltpu
from jax.sharding import PartitionSpec as P

ITERS = 2

HIGH = lax.Precision.HIGH


def angles_of(rows, columns, length):
    return 2.0 * np.pi * (np.outer(rows, columns) % length) / length


class Tables:
    def __init__(self, depth, rows, columns, space):
        half = columns // 2
        local = rows // space
        y = np.arange(columns)
        k = np.arange(half)
        ang = angles_of(y, k, columns)
        self.half = half
        real, imag = np.cos(ang), -np.sin(ang)
        self.col_fwd = np.concatenate([real, imag], 1)
        self.col_fwd_turned = np.concatenate([imag, -real], 1)
        weight = np.where(k == 0, 1.0, 2.0)[:, None]
        norm = 1.0 / (depth * rows * columns)
        back_real, back_imag = weight * np.cos(ang.T) * norm, -weight * np.sin(ang.T) * norm
        self.col_inv = np.concatenate([back_real, back_imag], 0)
        self.col_inv_turned = np.concatenate([-back_imag, back_real], 0)
        self.alternate = np.where(y % 2 == 0, 1.0, -1.0)
        self.norm = norm
        x = np.arange(rows)
        ang = angles_of(x, x, rows)
        self.row_cos, self.row_sin = np.cos(ang), np.sin(ang)
        edge = np.zeros((rows, space, columns))
        edge_inv = np.zeros((space, columns, rows))
        for s in range(space):
            ang = angles_of(x, np.arange(local) + s * local, rows)
            edge[:, s, :local] = np.cos(ang)
            edge[:, s, half : half + local] = -np.sin(ang)
            edge_inv[s, :local] = np.cos(ang.T) * norm
            edge_inv[s, half : half + local] = -np.sin(ang.T) * norm
        self.edge, self.edge_inv = edge, edge_inv
        z = np.arange(depth)
        ang = angles_of(z, z, depth)
        self.depth_cos, self.depth_sin = np.cos(ang), np.sin(ang)


def f32(table):
    return jnp.asarray(table, jnp.float32)


def dot(form, *operands):
    return jnp.einsum(form, *operands, precision=HIGH, preferred_element_type=jnp.float32)


def turned(lanes):
    half = lanes.shape[-1] // 2
    return jnp.concatenate([lanes[..., half:], -lanes[..., :half]], -1)


def slab_forward(t, space, volume):
    planes, rows, columns = volume.shape
    one = dot("zxy,yl->zxl", volume, f32(t.col_fwd))
    two = dot("zxy,yl->zxl", volume, f32(t.col_fwd_turned))
    main = dot("kx,zxl->kzl", f32(t.row_cos), one) + dot("kx,zxl->kzl", f32(t.row_sin), two)
    last = jnp.sum(volume * f32(t.alternate), -1)
    edge = dot("zx,xsl->szl", last, f32(t.edge))
    main = main.reshape(space, rows // space, planes, columns)
    return jnp.concatenate([main, edge[:, None]], 1)


def slab_inverse(t, spectrum):
    space, local, planes, columns = spectrum.shape
    main = spectrum[:, :-1].reshape(space * (local - 1), planes, columns)
    edge = spectrum[:, -1]
    one = dot("xk,kzl->zxl", f32(t.row_cos), main)
    two = dot("xk,kzl->zxl", f32(t.row_sin), main)
    last = dot("szl,slx->zx", edge, f32(t.edge_inv))
    return (
        dot("zxl,ly->zxy", one, f32(t.col_inv))
        - dot("zxl,ly->zxy", two, f32(t.col_inv_turned))
        + last[:, :, None] * f32(t.alternate)
    )


def depth_forward(t, lanes):
    return dot("kz,rzl->rkl", f32(t.depth_cos), lanes) + dot("kz,rzl->rkl", f32(t.depth_sin), turned(lanes))


def depth_inverse(t, lanes):
    return dot("zk,rkl->rzl", f32(t.depth_cos), lanes) - dot("zk,rkl->rzl", f32(t.depth_sin), turned(lanes))


def filtered(lanes, real, imag, sign):
    return lanes * real - sign * turned(lanes) * imag


def shards(estimate, observed, valid, psf_spectrum):
    space = lax.axis_size("space")
    views = lax.axis_size("view")
    planes, rows, columns = estimate.shape
    depth = planes * space
    local = rows // space
    half = columns // 2
    t = Tables(depth, rows, columns, space)
    view_count = observed.shape[0] * views
    shared = planes % views == 0
    share = planes // views if shared else planes

    psf = jnp.swapaxes(psf_spectrum[0], 1, 2)
    last = jnp.pad(jnp.swapaxes(psf[..., half], 1, 2), ((0, 0), (0, 0), (0, half - local)))
    psf = jnp.concatenate([psf[..., :half], last[:, None]], 1)
    psf = jnp.concatenate([psf, psf], -1)
    psf_real, psf_imag = psf[0], psf[1]

    def to_pencil(spectrum):
        parts = lax.all_to_all(spectrum, "space", 0, 0)
        return jnp.swapaxes(parts, 0, 1).reshape(local + 1, depth, columns)

    def to_slab(pencil):
        parts = jnp.swapaxes(pencil.reshape(local + 1, space, planes, columns), 0, 1)
        return lax.all_to_all(parts, "space", 0, 0)

    if shared:
        estimate = lax.dynamic_slice_in_dim(estimate, lax.axis_index("view") * share, share, 0)
    observed, valid = observed[0], valid[0].astype(jnp.float32)
    masked = valid * observed

    for iteration in range(ITERS):
        parts = lax.all_to_all(slab_forward(t, space, estimate), "space", 0, 0)
        if shared:
            parts = lax.all_gather(parts, "view")
            pencil = parts.transpose(2, 1, 0, 3, 4).reshape(local + 1, depth, columns)
        else:
            pencil = jnp.swapaxes(parts, 0, 1).reshape(local + 1, depth, columns)
        blurred = depth_inverse(t, filtered(depth_forward(t, pencil), psf_real, psf_imag, 1.0))
        ratio = masked / slab_inverse(t, to_slab(blurred)) + (1.0 - valid)
        pencil = to_pencil(slab_forward(t, space, ratio))
        correction = depth_inverse(t, filtered(depth_forward(t, pencil), psf_real, psf_imag, -1.0))
        if shared:
            correction = correction.reshape(local + 1, space, views, share, columns).transpose(2, 1, 0, 3, 4)
            correction = lax.psum_scatter(correction, "view", scatter_dimension=0)
            correction = lax.all_to_all(correction, "space", 0, 0)
        else:
            correction = to_slab(lax.psum(correction, "view"))
        estimate = estimate * slab_inverse(t, correction) / view_count
    if shared:
        estimate = lax.all_gather(estimate, "view", axis=0, tiled=True)
    return estimate


def split(value):
    high = value.astype(jnp.bfloat16)
    return high, (value - high.astype(jnp.float32)).astype(jnp.bfloat16)


def table_pair(table):
    high = np.asarray(table, np.float32).astype(jnp.bfloat16)
    low = (np.asarray(table, np.float32) - high.astype(np.float32)).astype(jnp.bfloat16)
    return jnp.asarray(np.stack([high, low]))


def product(left, right):
    form = functools.partial(jnp.dot, preferred_element_type=jnp.float32)
    return form(left[0], right[0]) + form(left[0], right[1]) + form(left[1], right[0])


def across(left, right):
    return lax.dot_general(
        left,
        right,
        (((1,), (1,)), ((), ())),
        precision=lax.Precision.HIGHEST,
        preferred_element_type=jnp.float32,
    )


def fourier(values, direction, turn):
    length = len(values)
    if length == 1:
        return list(values)
    radix = 4 if length % 4 == 0 else 2
    part = length // radix
    parts = [fourier(values[q::radix], direction, turn) for q in range(radix)]
    result = [None] * length
    for k in range(part):
        terms = []
        for q in range(radix):
            value = parts[q][k]
            if q * k:
                angle = 2.0 * np.pi * q * k / length
                if 8 * q * k == length:
                    value = (value + direction * turn(value)) * float(np.cos(angle))
                else:
                    value = value * float(np.cos(angle)) + turn(value) * float(direction * np.sin(angle))
            terms.append(value)
        if radix == 2:
            result[k], result[k + part] = terms[0] + terms[1], terms[0] - terms[1]
            continue
        even, odd = terms[0] + terms[2], terms[1] + terms[3]
        even_less, odd_less = terms[0] - terms[2], turn(terms[1] - terms[3])
        result[k], result[k + 2 * part] = even + odd, even - odd
        one, three = even_less + odd_less, even_less - odd_less
        result[k + part], result[k + 3 * part] = (one, three) if direction > 0 else (three, one)
    return result


def iterations_kernel(
    sizes, est, observed, valid, psf, psf_last, col_fwd, col_inv, row_fwd, row_inv, edge, edge_back,
    dep_last_fwd, dep_last_inv, out,
    now, a_send, a_recv, b_send, b_recv, c_send, c_recv, d_send, d_recv, e_send, e_recv,
    a_sems, g_sems, b_sems, c_sems, d_sems, e_sems, o_sems,
):
    space, views, planes, share, rows, columns, depth = sizes
    local = rows // space
    half = columns // 2
    block = share * local + 8
    me = lax.axis_index("space")
    view = lax.axis_index("view")
    hops = []
    hop = views // 2
    while hop:
        hops.append(hop)
        hop //= 2

    def partner(hop, index):
        return index + hop - 2 * hop * ((index // hop) % 2)

    def peer(step):
        return lax.rem(me + step, space)

    def part(index, count=1):
        return pl.ds(pl.multiple_of(index * block, 8), count * block)

    barrier = pltpu.get_barrier_semaphore()
    for step in range(1, space):
        pl.semaphore_signal(barrier, inc=1, device_id={"space": peer(step)}, device_id_type=pl.DeviceIdType.MESH)
    for hop in hops:
        pl.semaphore_signal(barrier, inc=1, device_id={"view": partner(hop, view)}, device_id_type=pl.DeviceIdType.MESH)

    lane = lax.broadcasted_iota(jnp.int32, (8, columns), 1)
    line = lax.broadcasted_iota(jnp.int32, (8, columns), 0)
    alternate = jnp.where(lane % 2 == 0, 1.0, -1.0).astype(jnp.float32)
    sign = jnp.where(lane[:1] < half, 1.0, -1.0).astype(jnp.float32)

    def turn(value):
        return pltpu.roll(value, half, 1) * sign

    def alternate_of(plane):
        return jnp.where(line == plane, alternate, 0.0)

    def forward_plane(volume, store, plane, base, chunks):
        one = product(split(volume), (col_fwd[0], col_fwd[1]))
        both = jnp.concatenate([one[:, :columns], one[:, columns:]], 0)
        main = product((row_fwd[0], row_fwd[1]), split(both))
        for j in range(space):
            start = pl.multiple_of((j * chunks + base) * block + plane * local, 8)
            store[pl.ds(start, local), :] = main[j * local : (j + 1) * local]
        return across(alternate_of(plane), volume)

    def forward_last(sums, store, base, chunks):
        last = jnp.dot(sums, edge[...], precision=lax.Precision.HIGHEST, preferred_element_type=jnp.float32)
        for j in range(space):
            start = pl.multiple_of((j * chunks + base) * block + share * local, 8)
            store[pl.ds(start, 8), :] = last[:, j * columns : (j + 1) * columns]

    def inverse_last(held, base, chunks):
        last = jnp.concatenate(
            [held[pl.ds(pl.multiple_of((j * chunks + base) * block + share * local, 8), 8), :] for j in range(space)], 1
        )
        return across(edge_back[...], last)

    def inverse_plane(held, last, plane, base, chunks):
        main = jnp.concatenate(
            [
                held[pl.ds(pl.multiple_of((j * chunks + base) * block + plane * local, 8), local), :]
                for j in range(space)
            ],
            0,
        )
        both = product((row_inv[0], row_inv[1]), split(main))
        both = jnp.concatenate([both[:rows], both[rows:]], 1)
        value = product(split(both), (col_inv[0], col_inv[1]))
        return value + jnp.dot(
            last, alternate_of(plane), precision=lax.Precision.HIGHEST, preferred_element_type=jnp.float32
        )

    def filtered_pencil(held, store, conjugate):
        count = space * views
        left = lax.broadcasted_iota(jnp.int32, (1, columns), 1) < half

        def middle(value, real, imag):
            return value * real - (conjugate * turn(value)) * imag

        def doubled(start):
            value = psf[pl.ds(pl.multiple_of(start, 8), 8), :]
            return jnp.where(left, value, pltpu.roll(value, half, 1))

        def group(g, carry):
            row = pl.multiple_of(g * 8, 8)

            def place(z):
                return pl.ds((z // share) * block + (z % share) * local + row, 8)

            values = fourier([held[place(z), :] for z in range(depth)], 1.0, turn)
            for k in range(depth):
                values[k] = middle(
                    values[k], doubled(k * local + row), doubled((depth + k) * local + row)
                )
            values = fourier(values, -1.0, turn)
            for z in range(depth):
                store[place(z), :] = values[z]
            return carry

        lax.fori_loop(0, local // 8, group, 0)
        last = jnp.concatenate(
            [held[q * block + share * local : q * block + share * local + 8, :] for q in range(count)], 0
        )
        last = jnp.concatenate([last, turn(last)], 0)
        last = jnp.dot(
            dep_last_fwd[...], last, precision=lax.Precision.HIGHEST, preferred_element_type=jnp.float32
        )
        last = middle(last, psf_last[0], psf_last[1])
        last = jnp.concatenate([last, turn(last)], 0)
        last = jnp.dot(
            dep_last_inv[...], last, precision=lax.Precision.HIGHEST, preferred_element_type=jnp.float32
        )
        for q in range(count):
            store[q * block + share * local : q * block + share * local + 8, :] = last[q * 8 : (q + 1) * 8]

    def remote(source, target, sems, index, **device):
        return pltpu.make_async_remote_copy(
            src_ref=source,
            dst_ref=target,
            send_sem=sems.at[(0,) + index],
            recv_sem=sems.at[(1,) + index],
            device_id=device,
            device_id_type=pl.DeviceIdType.MESH,
        )

    def iteration(index, carry):
        def estimate_plane(plane, sums):
            return sums + forward_plane(now[plane], a_send, plane, 0, 1)

        sums = lax.fori_loop(0, share, estimate_plane, jnp.zeros((8, rows), jnp.float32))
        forward_last(sums, a_send, 0, 1)
        spread = []
        for step in range(1, space):
            j = peer(step)
            copy = remote(a_send.at[part(j)], a_recv.at[part(me * views + view)], a_sems, (step,), space=j)
            copy.start()
            spread.append(copy)
        a_recv[part(me * views + view), :] = a_send[part(me), :]
        held = [0]
        for level, hop in enumerate(hops):
            arrived = []
            for step in range(space):
                source = lax.rem(me - step + space, space)
                if level == 0 and step:
                    spread[step - 1].wait()
                for order, offset in enumerate(held):
                    owner = view
                    for other in hops:
                        if offset & other:
                            owner = partner(other, owner)
                    where = part(source * views + owner)
                    copy = remote(
                        a_recv.at[where], a_recv.at[where], g_sems, (level, step, order), view=partner(hop, view)
                    )
                    copy.start()
                    arrived.append(copy)
            for copy in arrived:
                copy.wait()
            held = held + [offset | hop for offset in held]

        filtered_pencil(a_recv, b_send, 1.0)

        sent = []
        for chunk in range(views):
            for step in range(1, space):
                j = peer(step)
                copy = remote(
                    b_send.at[part(j * views + chunk)], b_recv.at[part(me * views + chunk)], b_sems, (chunk, step), space=j
                )
                copy.start()
                sent.append(copy)
        ratios = []
        for chunk in range(views):
            b_recv[part(me * views + chunk), :] = b_send[part(me * views + chunk), :]
            for step in range(1, space):
                sent[chunk * (space - 1) + step - 1].wait()
            last = inverse_last(b_recv, chunk, views)

            def ratio_plane(plane, sums, chunk=chunk, last=last):
                blurred = inverse_plane(b_recv, last, plane, chunk, views)
                mask = valid[chunk * share + plane].astype(jnp.float32)
                ratio = mask * observed[chunk * share + plane] / blurred + (1.0 - mask)
                return sums + forward_plane(ratio, c_send, plane, chunk, views)

            sums = lax.fori_loop(0, share, ratio_plane, jnp.zeros((8, rows), jnp.float32))
            forward_last(sums, c_send, chunk, views)
            c_recv[part(me * views + chunk), :] = c_send[part(me * views + chunk), :]
            for step in range(1, space):
                j = peer(step)
                copy = remote(
                    c_send.at[part(j * views + chunk)], c_recv.at[part(me * views + chunk)], c_sems, (chunk, step), space=j
                )
                copy.start()
                ratios.append(copy)
        for copy in ratios:
            copy.wait()

        filtered_pencil(c_recv, d_send, -1.0)

        kept = [0]
        for hop in hops:
            kept = kept + [offset | hop for offset in kept]

        def chunk_of(offset):
            owner = view
            for other in hops:
                if offset & other:
                    owner = partner(other, owner)
            return owner

        shares = []
        for level, hop in enumerate(reversed(hops)):
            copies = []
            keep = [offset for offset in kept if not offset & hop]
            for order, offset in enumerate(keep):
                for step in range(space):
                    place = part(peer(step + 1) * views + chunk_of(offset | hop))
                    copy = remote(
                        d_send.at[place],
                        d_recv.at[part((level * views + order) * space + step)],
                        d_sems,
                        (level, order, step),
                        view=partner(hop, view),
                    )
                    copy.start()
                    copies.append(copy)
            for order, offset in enumerate(keep):
                for step in range(space):
                    copies[order * space + step].wait()
                    j = peer(step + 1)
                    place = part(j * views + chunk_of(offset))
                    extra = d_recv[part((level * views + order) * space + step), :]
                    if hop != hops[0]:
                        d_send[place, :] = d_send[place, :] + extra
                    elif step == space - 1:
                        e_recv[part(me), :] = d_send[place, :] + extra
                    else:
                        e_send[part(step), :] = d_send[place, :] + extra
                        copy = remote(e_send.at[part(step)], e_recv.at[part(me)], e_sems, (step,), space=j)
                        copy.start()
                        shares.append(copy)
            kept = keep
        for copy in shares:
            copy.wait()
        last = inverse_last(e_recv, 0, 1)

        def update_plane(plane, carry):
            now[plane] = now[plane] * inverse_plane(e_recv, last, plane, 0, 1) * (1.0 / views)
            return carry

        lax.fori_loop(0, share, update_plane, 0)
        return carry

    now[...] = est[...]
    pl.semaphore_wait(barrier, space - 1 + len(hops))
    lax.fori_loop(0, ITERS, iteration, 0)

    def planes_of(owner):
        return pl.ds(owner * share, share)

    out[planes_of(view)] = now[...]
    owners = [view]
    for level, hop in enumerate(hops):
        copies = []
        for order, owner in enumerate(owners):
            where = planes_of(owner)
            copy = remote(out.at[where], out.at[where], o_sems, (level, order), view=partner(hop, view))
            copy.start()
            copies.append(copy)
        for copy in copies:
            copy.wait()
        owners = owners + [partner(hop, owner) for owner in owners]


def kernel_tables(t, space, views, share):
    planes = share * views
    depth = planes * space
    place = (np.arange(space * views)[:, None] * 8 + np.arange(share)[None, :]).reshape(-1)
    last_cos = np.zeros((depth, space * views * 8))
    last_sin = np.zeros((depth, space * views * 8))
    last_cos[:, place] = t.depth_cos
    last_sin[:, place] = t.depth_sin
    return (
        table_pair(np.concatenate([t.col_fwd, t.col_fwd_turned], 1)),
        table_pair(np.concatenate([t.col_inv, -t.col_inv_turned], 0)),
        table_pair(np.concatenate([t.row_cos, t.row_sin], 1)),
        table_pair(np.concatenate([t.row_cos, t.row_sin], 0)),
        f32(t.edge.reshape(t.edge.shape[0], -1)),
        f32(t.edge_inv.transpose(2, 0, 1).reshape(t.edge.shape[0], -1)),
        f32(np.concatenate([last_cos, last_sin], 1)),
        f32(np.concatenate([last_cos.T, -last_sin.T], 1)),
    )


def kernel_shards(estimate, observed, valid, psf_spectrum):
    space = lax.axis_size("space")
    views = lax.axis_size("view")
    planes, rows, columns = estimate.shape
    depth = planes * space
    local = rows // space
    half = columns // 2
    share = planes // views
    block = share * local + 8
    t = Tables(depth, rows, columns, space)
    tables = kernel_tables(t, space, views, share)
    last = jnp.sum(jnp.where(jnp.arange(columns) == half, psf_spectrum[0], 0.0), -1)
    last = jnp.pad(last, ((0, 0), (0, 0), (0, half - local)))
    last = jnp.concatenate([last, last], -1)
    psf = psf_spectrum.reshape(2 * depth * local, columns)
    estimate = lax.dynamic_slice_in_dim(estimate, lax.axis_index("view") * share, share, 0)
    levels = max(views.bit_length() - 1, 1)
    big = pltpu.VMEM((space * views * block, columns), jnp.float32)
    small = pltpu.VMEM((space * block, columns), jnp.float32)
    operands = (observed[0], valid[0], psf, last) + tables
    call = pl.pallas_call(
        functools.partial(iterations_kernel, (space, views, planes, share, rows, columns, depth)),
        out_shape=jax.ShapeDtypeStruct((planes, rows, columns), jnp.float32),
        in_specs=[pl.BlockSpec(memory_space=pltpu.VMEM)] * (len(operands) + 1),
        out_specs=pl.BlockSpec(memory_space=pltpu.VMEM),
        scratch_shapes=[
            pltpu.VMEM(estimate.shape, jnp.float32),
            small, big, big, big, big, big, big,
            pltpu.VMEM((levels * views * space * block, columns), jnp.float32),
            small, small,
            pltpu.SemaphoreType.DMA((2, space)),
            pltpu.SemaphoreType.DMA((2, levels, space, views)),
            pltpu.SemaphoreType.DMA((2, views, space)),
            pltpu.SemaphoreType.DMA((2, views, space)),
            pltpu.SemaphoreType.DMA((2, levels, views, space)),
            pltpu.SemaphoreType.DMA((2, space)),
            pltpu.SemaphoreType.DMA((2, levels, views)),
        ],
        compiler_params=pltpu.CompilerParams(
            collective_id=0, has_side_effects=True, vmem_limit_bytes=56 * 1024 * 1024
        ),
        name="iterations",
    )
    return call(estimate, *operands)


def fits(mesh, estimate, observed):
    space, views = mesh.shape["space"], mesh.shape["view"]
    planes = estimate.shape[0] // space
    local = observed.shape[2] // mesh.shape["blocks"] // space
    return (
        planes % views == 0
        and planes // views <= 8
        and local % 8 == 0
        and views > 1
        and views & (views - 1) == 0
        and observed.shape[0] == views
    )


def solution(mesh):
    def mapped(body):
        return jax.shard_map(
            body,
            mesh=mesh,
            in_specs=(
                P("space", "blocks", None),
                P("view", "space", "blocks", None),
                P("view", "space", "blocks", None),
                P("view", None, None, "space", None),
            ),
            out_specs=P("space", "blocks", None),
            check_vma=False,
        )

    def refine(estimate, observed, valid, psf_spectrum):
        body = kernel_shards if fits(mesh, estimate, observed) else shards
        return mapped(body)(estimate, observed, valid, psf_spectrum)

    return refine
```

```python
import functools

import numpy as np

import jax
import jax.numpy as jnp
from jax import lax
from jax.experimental import pallas as pl
from jax.experimental.pallas import tpu as pltpu
from jax.sharding import PartitionSpec as P

ITERS = 2

HIGH = lax.Precision.HIGH


def angles_of(rows, columns, length):
    return 2.0 * np.pi * (np.outer(rows, columns) % length) / length


class Tables:
    def __init__(self, depth, rows, columns, space):
        half = columns // 2
        local = rows // space
        y = np.arange(columns)
        k = np.arange(half)
        ang = angles_of(y, k, columns)
        self.half = half
        real, imag = np.cos(ang), -np.sin(ang)
        self.col_fwd = np.concatenate([real, imag], 1)
        self.col_fwd_turned = np.concatenate([imag, -real], 1)
        weight = np.where(k == 0, 1.0, 2.0)[:, None]
        norm = 1.0 / (depth * rows * columns)
        back_real, back_imag = weight * np.cos(ang.T) * norm, -weight * np.sin(ang.T) * norm
        self.col_inv = np.concatenate([back_real, back_imag], 0)
        self.col_inv_turned = np.concatenate([-back_imag, back_real], 0)
        self.alternate = np.where(y % 2 == 0, 1.0, -1.0)
        self.norm = norm
        x = np.arange(rows)
        ang = angles_of(x, x, rows)
        self.row_cos, self.row_sin = np.cos(ang), np.sin(ang)
        edge = np.zeros((rows, space, columns))
        edge_inv = np.zeros((space, columns, rows))
        for s in range(space):
            ang = angles_of(x, np.arange(local) + s * local, rows)
            edge[:, s, :local] = np.cos(ang)
            edge[:, s, half : half + local] = -np.sin(ang)
            edge_inv[s, :local] = np.cos(ang.T) * norm
            edge_inv[s, half : half + local] = -np.sin(ang.T) * norm
        self.edge, self.edge_inv = edge, edge_inv
        z = np.arange(depth)
        ang = angles_of(z, z, depth)
        self.depth_cos, self.depth_sin = np.cos(ang), np.sin(ang)


def f32(table):
    return jnp.asarray(table, jnp.float32)


def dot(form, *operands):
    return jnp.einsum(form, *operands, precision=HIGH, preferred_element_type=jnp.float32)


def turned(lanes):
    half = lanes.shape[-1] // 2
    return jnp.concatenate([lanes[..., half:], -lanes[..., :half]], -1)


def slab_forward(t, space, volume):
    planes, rows, columns = volume.shape
    one = dot("zxy,yl->zxl", volume, f32(t.col_fwd))
    two = dot("zxy,yl->zxl", volume, f32(t.col_fwd_turned))
    main = dot("kx,zxl->kzl", f32(t.row_cos), one) + dot("kx,zxl->kzl", f32(t.row_sin), two)
    last = jnp.sum(volume * f32(t.alternate), -1)
    edge = dot("zx,xsl->szl", last, f32(t.edge))
    main = main.reshape(space, rows // space, planes, columns)
    return jnp.concatenate([main, edge[:, None]], 1)


def slab_inverse(t, spectrum):
    space, local, planes, columns = spectrum.shape
    main = spectrum[:, :-1].reshape(space * (local - 1), planes, columns)
    edge = spectrum[:, -1]
    one = dot("xk,kzl->zxl", f32(t.row_cos), main)
    two = dot("xk,kzl->zxl", f32(t.row_sin), main)
    last = dot("szl,slx->zx", edge, f32(t.edge_inv))
    return (
        dot("zxl,ly->zxy", one, f32(t.col_inv))
        - dot("zxl,ly->zxy", two, f32(t.col_inv_turned))
        + last[:, :, None] * f32(t.alternate)
    )


def depth_forward(t, lanes):
    return dot("kz,rzl->rkl", f32(t.depth_cos), lanes) + dot("kz,rzl->rkl", f32(t.depth_sin), turned(lanes))


def depth_inverse(t, lanes):
    return dot("zk,rkl->rzl", f32(t.depth_cos), lanes) - dot("zk,rkl->rzl", f32(t.depth_sin), turned(lanes))


def filtered(lanes, real, imag, sign):
    return lanes * real - sign * turned(lanes) * imag


def shards(estimate, observed, valid, psf_spectrum):
    space = lax.axis_size("space")
    views = lax.axis_size("view")
    planes, rows, columns = estimate.shape
    depth = planes * space
    local = rows // space
    half = columns // 2
    t = Tables(depth, rows, columns, space)
    view_count = observed.shape[0] * views
    shared = planes % views == 0
    share = planes // views if shared else planes

    psf = jnp.swapaxes(psf_spectrum[0], 1, 2)
    last = jnp.pad(jnp.swapaxes(psf[..., half], 1, 2), ((0, 0), (0, 0), (0, half - local)))
    psf = jnp.concatenate([psf[..., :half], last[:, None]], 1)
    psf = jnp.concatenate([psf, psf], -1)
    psf_real, psf_imag = psf[0], psf[1]

    def to_pencil(spectrum):
        parts = lax.all_to_all(spectrum, "space", 0, 0)
        return jnp.swapaxes(parts, 0, 1).reshape(local + 1, depth, columns)

    def to_slab(pencil):
        parts = jnp.swapaxes(pencil.reshape(local + 1, space, planes, columns), 0, 1)
        return lax.all_to_all(parts, "space", 0, 0)

    if shared:
        estimate = lax.dynamic_slice_in_dim(estimate, lax.axis_index("view") * share, share, 0)
    observed, valid = observed[0], valid[0].astype(jnp.float32)
    masked = valid * observed

    for iteration in range(ITERS):
        parts = lax.all_to_all(slab_forward(t, space, estimate), "space", 0, 0)
        if shared:
            parts = lax.all_gather(parts, "view")
            pencil = parts.transpose(2, 1, 0, 3, 4).reshape(local + 1, depth, columns)
        else:
            pencil = jnp.swapaxes(parts, 0, 1).reshape(local + 1, depth, columns)
        blurred = depth_inverse(t, filtered(depth_forward(t, pencil), psf_real, psf_imag, 1.0))
        ratio = masked / slab_inverse(t, to_slab(blurred)) + (1.0 - valid)
        pencil = to_pencil(slab_forward(t, space, ratio))
        correction = depth_inverse(t, filtered(depth_forward(t, pencil), psf_real, psf_imag, -1.0))
        if shared:
            correction = correction.reshape(local + 1, space, views, share, columns).transpose(2, 1, 0, 3, 4)
            correction = lax.psum_scatter(correction, "view", scatter_dimension=0)
            correction = lax.all_to_all(correction, "space", 0, 0)
        else:
            correction = to_slab(lax.psum(correction, "view"))
        estimate = estimate * slab_inverse(t, correction) / view_count
    if shared:
        estimate = lax.all_gather(estimate, "view", axis=0, tiled=True)
    return estimate


def split(value):
    high = value.astype(jnp.bfloat16)
    return high, (value - high.astype(jnp.float32)).astype(jnp.bfloat16)


def table_pair(table):
    high = np.asarray(table, np.float32).astype(jnp.bfloat16)
    low = (np.asarray(table, np.float32) - high.astype(np.float32)).astype(jnp.bfloat16)
    return jnp.asarray(np.stack([high, low]))


def product(left, right):
    form = functools.partial(jnp.dot, preferred_element_type=jnp.float32)
    return form(left[0], right[0]) + form(left[0], right[1]) + form(left[1], right[0])


def across(left, right):
    return lax.dot_general(
        left,
        right,
        (((1,), (1,)), ((), ())),
        preferred_element_type=jnp.float32,
    )


def fourier(values, direction, turn):
    length = len(values)
    if length == 1:
        return list(values)
    radix = 4 if length % 4 == 0 else 2
    part = length // radix
    parts = [fourier(values[q::radix], direction, turn) for q in range(radix)]
    result = [None] * length
    for k in range(part):
        terms = []
        for q in range(radix):
            value = parts[q][k]
            if q * k:
                angle = 2.0 * np.pi * q * k / length
                if 8 * q * k == length:
                    value = (value + direction * turn(value)) * float(np.cos(angle))
                else:
                    value = value * float(np.cos(angle)) + turn(value) * float(direction * np.sin(angle))
            terms.append(value)
        if radix == 2:
            result[k], result[k + part] = terms[0] + terms[1], terms[0] - terms[1]
            continue
        even, odd = terms[0] + terms[2], terms[1] + terms[3]
        even_less, odd_less = terms[0] - terms[2], turn(terms[1] - terms[3])
        result[k], result[k + 2 * part] = even + odd, even - odd
        one, three = even_less + odd_less, even_less - odd_less
        result[k + part], result[k + 3 * part] = (one, three) if direction > 0 else (three, one)
    return result


def iterations_kernel(
    sizes, est, observed, valid, psf, psf_last, col_fwd, col_inv, row_fwd, row_inv, edge, edge_back,
    dep_last_fwd, dep_last_inv, out,
    now, a_send, a_recv, b_send, b_recv, c_send, c_recv, d_send, d_recv, e_send, e_recv,
    a_sems, g_sems, b_sems, c_sems, d_sems, e_sems, o_sems,
):
    space, views, planes, share, rows, columns, depth = sizes
    local = rows // space
    half = columns // 2
    block = share * local + 8
    me = lax.axis_index("space")
    view = lax.axis_index("view")
    hops = []
    hop = views // 2
    while hop:
        hops.append(hop)
        hop //= 2

    def partner(hop, index):
        return index + hop - 2 * hop * ((index // hop) % 2)

    def peer(step):
        return lax.rem(me + step, space)

    def part(index, count=1):
        return pl.ds(pl.multiple_of(index * block, 8), count * block)

    barrier = pltpu.get_barrier_semaphore()
    for step in range(1, space):
        pl.semaphore_signal(barrier, inc=1, device_id={"space": peer(step)}, device_id_type=pl.DeviceIdType.MESH)
    for hop in hops:
        pl.semaphore_signal(barrier, inc=1, device_id={"view": partner(hop, view)}, device_id_type=pl.DeviceIdType.MESH)

    lane = lax.broadcasted_iota(jnp.int32, (8, columns), 1)
    sign = jnp.where(lane[:1] < half, 1.0, -1.0).astype(jnp.float32)

    def turn(value):
        return pltpu.roll(value, half, 1) * sign

    lanes = lax.broadcasted_iota(jnp.int32, (1, columns), 1)
    pair = 2 if share % 2 == 0 else 1

    def rows_of(index, plane):
        return pl.ds(pl.multiple_of(index * block + plane * local, 8), local)

    def rows_of_last(index):
        return pl.ds(pl.multiple_of(index * block + share * local, 8), 8)

    def forward_planes(volumes, store, plane, sums, base, chunks):
        both = product(split(jnp.concatenate(volumes, 0)), (col_fwd[0], col_fwd[1]))
        upper, lower = [], []
        for i in range(len(volumes)):
            first = both[i * rows : (i + 1) * rows, :columns]
            sums = jnp.where(lanes == plane + i, first[:, half : half + 1], sums)
            upper.append(jnp.where(lanes == half, 0.0, first))
            lower.append(both[i * rows : (i + 1) * rows, columns:])
        both = jnp.concatenate([jnp.concatenate(upper, 1), jnp.concatenate(lower, 1)], 0)
        main = product((row_fwd[0], row_fwd[1]), split(both))
        for i in range(len(volumes)):
            for j in range(space):
                store[rows_of(j * chunks + base, plane + i), :] = main[
                    j * local : (j + 1) * local, i * columns : (i + 1) * columns
                ]
        return sums

    def forward_last(sums, store, base, chunks):
        last = product(split(jnp.transpose(sums)[:16]), (edge[0], edge[1]))
        for j in range(space):
            store[rows_of_last(j * chunks + base), :] = last[:8, j * columns : (j + 1) * columns]

    def inverse_last(held, base, chunks):
        last = jnp.concatenate([held[rows_of_last(j * chunks + base), :] for j in range(space)], 1)
        last = split(jnp.concatenate([last, jnp.zeros((columns - 8, space * columns), jnp.float32)], 0))
        return across(edge_back[0], last[0]) + across(edge_back[0], last[1]) + across(edge_back[1], last[0])

    def inverse_planes(held, last, plane, base, chunks):
        main = jnp.concatenate(
            [
                jnp.concatenate([held[rows_of(j * chunks + base, plane + i), :] for j in range(space)], 0)
                for i in range(pair)
            ],
            1,
        )
        both = product((row_inv[0], row_inv[1]), split(main))
        stacked = []
        for i in range(pair):
            first = both[:rows, i * columns : (i + 1) * columns]
            picked = jnp.sum(jnp.where(lanes == plane + i, last, 0.0), axis=1, keepdims=True)
            first = jnp.where(lanes == half, picked, first)
            stacked.append(jnp.concatenate([first, both[rows:, i * columns : (i + 1) * columns]], 1))
        return product(split(jnp.concatenate(stacked, 0)), (col_inv[0], col_inv[1]))

    def filtered_pencil(held, store, conjugate):
        count = space * views
        left = lax.broadcasted_iota(jnp.int32, (1, columns), 1) < half

        def middle(value, real, imag):
            return value * real - (conjugate * turn(value)) * imag

        def doubled(start):
            value = psf[pl.ds(pl.multiple_of(start, 8), 8), :]
            return jnp.where(left, value, pltpu.roll(value, half, 1))

        def group(g, carry):
            row = pl.multiple_of(g * 8, 8)

            def place(z):
                return pl.ds((z // share) * block + (z % share) * local + row, 8)

            values = fourier([held[place(z), :] for z in range(depth)], 1.0, turn)
            for k in range(depth):
                values[k] = middle(
                    values[k], doubled(k * local + row), doubled((depth + k) * local + row)
                )
            values = fourier(values, -1.0, turn)
            for z in range(depth):
                store[place(z), :] = values[z]
            return carry

        lax.fori_loop(0, local // 8, group, 0)
        last = jnp.concatenate(
            [held[q * block + share * local : q * block + share * local + 8, :] for q in range(count)], 0
        )
        last = jnp.concatenate([last, turn(last)], 0)
        last = jnp.dot(
            dep_last_fwd[...], last, precision=lax.Precision.HIGHEST, preferred_element_type=jnp.float32
        )
        last = middle(last, psf_last[0], psf_last[1])
        last = jnp.concatenate([last, turn(last)], 0)
        last = jnp.dot(
            dep_last_inv[...], last, precision=lax.Precision.HIGHEST, preferred_element_type=jnp.float32
        )
        for q in range(count):
            store[q * block + share * local : q * block + share * local + 8, :] = last[q * 8 : (q + 1) * 8]

    def remote(source, target, sems, index, **device):
        return pltpu.make_async_remote_copy(
            src_ref=source,
            dst_ref=target,
            send_sem=sems.at[(0,) + index],
            recv_sem=sems.at[(1,) + index],
            device_id=device,
            device_id_type=pl.DeviceIdType.MESH,
        )

    def iteration(index, carry):
        def estimate_planes(turn_index, sums):
            plane = turn_index * pair
            return forward_planes([now[plane + i] for i in range(pair)], a_send, plane, sums, 0, 1)

        sums = lax.fori_loop(0, share // pair, estimate_planes, jnp.zeros((rows, columns), jnp.float32))
        forward_last(sums, a_send, 0, 1)
        spread = []
        for step in range(1, space):
            j = peer(step)
            copy = remote(a_send.at[part(j)], a_recv.at[part(me * views + view)], a_sems, (step,), space=j)
            copy.start()
            spread.append(copy)
        a_recv[part(me * views + view), :] = a_send[part(me), :]
        held = [0]
        for level, hop in enumerate(hops):
            arrived = []
            for step in range(space):
                source = lax.rem(me - step + space, space)
                if level == 0 and step:
                    spread[step - 1].wait()
                for order, offset in enumerate(held):
                    owner = view
                    for other in hops:
                        if offset & other:
                            owner = partner(other, owner)
                    where = part(source * views + owner)
                    copy = remote(
                        a_recv.at[where], a_recv.at[where], g_sems, (level, step, order), view=partner(hop, view)
                    )
                    copy.start()
                    arrived.append(copy)
            for copy in arrived:
                copy.wait()
            held = held + [offset | hop for offset in held]

        filtered_pencil(a_recv, b_send, 1.0)

        sent = []
        for chunk in range(views):
            for step in range(1, space):
                j = peer(step)
                copy = remote(
                    b_send.at[part(j * views + chunk)], b_recv.at[part(me * views + chunk)], b_sems, (chunk, step), space=j
                )
                copy.start()
                sent.append(copy)
        ratios = []
        for chunk in range(views):
            b_recv[part(me * views + chunk), :] = b_send[part(me * views + chunk), :]
            for step in range(1, space):
                sent[chunk * (space - 1) + step - 1].wait()
            last = inverse_last(b_recv, chunk, views)

            def ratio_planes(turn_index, sums, chunk=chunk, last=last):
                plane = turn_index * pair
                blurred = inverse_planes(b_recv, last, plane, chunk, views)
                ratios = []
                for i in range(pair):
                    mask = valid[chunk * share + plane + i].astype(jnp.float32)
                    masked = mask * observed[chunk * share + plane + i]
                    ratios.append(masked / blurred[i * rows : (i + 1) * rows] + (1.0 - mask))
                return forward_planes(ratios, c_send, plane, sums, chunk, views)

            sums = lax.fori_loop(0, share // pair, ratio_planes, jnp.zeros((rows, columns), jnp.float32))
            forward_last(sums, c_send, chunk, views)
            c_recv[part(me * views + chunk), :] = c_send[part(me * views + chunk), :]
            for step in range(1, space):
                j = peer(step)
                copy = remote(
                    c_send.at[part(j * views + chunk)], c_recv.at[part(me * views + chunk)], c_sems, (chunk, step), space=j
                )
                copy.start()
                ratios.append(copy)
        for copy in ratios:
            copy.wait()

        filtered_pencil(c_recv, d_send, -1.0)

        kept = [0]
        for hop in hops:
            kept = kept + [offset | hop for offset in kept]

        def chunk_of(offset):
            owner = view
            for other in hops:
                if offset & other:
                    owner = partner(other, owner)
            return owner

        shares = []
        for level, hop in enumerate(reversed(hops)):
            copies = []
            keep = [offset for offset in kept if not offset & hop]
            for order, offset in enumerate(keep):
                for step in range(space):
                    place = part(peer(step + 1) * views + chunk_of(offset | hop))
                    copy = remote(
                        d_send.at[place],
                        d_recv.at[part((level * views + order) * space + step)],
                        d_sems,
                        (level, order, step),
                        view=partner(hop, view),
                    )
                    copy.start()
                    copies.append(copy)
            for order, offset in enumerate(keep):
                for step in range(space):
                    copies[order * space + step].wait()
                    j = peer(step + 1)
                    place = part(j * views + chunk_of(offset))
                    extra = d_recv[part((level * views + order) * space + step), :]
                    if hop != hops[0]:
                        d_send[place, :] = d_send[place, :] + extra
                    elif step == space - 1:
                        e_recv[part(me), :] = d_send[place, :] + extra
                    else:
                        e_send[part(step), :] = d_send[place, :] + extra
                        copy = remote(e_send.at[part(step)], e_recv.at[part(me)], e_sems, (step,), space=j)
                        copy.start()
                        shares.append(copy)
            kept = keep
        for copy in shares:
            copy.wait()
        last = inverse_last(e_recv, 0, 1)

        def update_planes(turn_index, carry):
            plane = turn_index * pair
            value = inverse_planes(e_recv, last, plane, 0, 1)
            for i in range(pair):
                now[plane + i] = now[plane + i] * value[i * rows : (i + 1) * rows] * (1.0 / views)
            return carry

        lax.fori_loop(0, share // pair, update_planes, 0)
        return carry

    now[...] = est[...]
    pl.semaphore_wait(barrier, space - 1 + len(hops))
    lax.fori_loop(0, ITERS, iteration, 0)

    def planes_of(owner):
        return pl.ds(owner * share, share)

    out[planes_of(view)] = now[...]
    owners = [view]
    for level, hop in enumerate(hops):
        copies = []
        for order, owner in enumerate(owners):
            where = planes_of(owner)
            copy = remote(out.at[where], out.at[where], o_sems, (level, order), view=partner(hop, view))
            copy.start()
            copies.append(copy)
        for copy in copies:
            copy.wait()
        owners = owners + [partner(hop, owner) for owner in owners]


def kernel_tables(t, space, views, share):
    planes = share * views
    depth = planes * space
    place = (np.arange(space * views)[:, None] * 8 + np.arange(share)[None, :]).reshape(-1)
    last_cos = np.zeros((depth, space * views * 8))
    last_sin = np.zeros((depth, space * views * 8))
    last_cos[:, place] = t.depth_cos
    last_sin[:, place] = t.depth_sin
    col_fwd = np.concatenate([t.col_fwd, t.col_fwd_turned], 1)
    col_fwd[:, t.half] = t.alternate
    col_inv = np.concatenate([t.col_inv, -t.col_inv_turned], 0)
    col_inv[t.half] = t.alternate
    return (
        table_pair(col_fwd),
        table_pair(col_inv),
        table_pair(np.concatenate([t.row_cos, t.row_sin], 1)),
        table_pair(np.concatenate([t.row_cos, t.row_sin], 0)),
        table_pair(t.edge.reshape(t.edge.shape[0], -1)),
        table_pair(t.edge_inv.transpose(2, 0, 1).reshape(t.edge.shape[0], -1)),
        f32(np.concatenate([last_cos, last_sin], 1)),
        f32(np.concatenate([last_cos.T, -last_sin.T], 1)),
    )


def kernel_shards(estimate, observed, valid, psf_spectrum):
    space = lax.axis_size("space")
    views = lax.axis_size("view")
    planes, rows, columns = estimate.shape
    depth = planes * space
    local = rows // space
    half = columns // 2
    share = planes // views
    block = share * local + 8
    t = Tables(depth, rows, columns, space)
    tables = kernel_tables(t, space, views, share)
    last = jnp.sum(jnp.where(jnp.arange(columns) == half, psf_spectrum[0], 0.0), -1)
    last = jnp.pad(last, ((0, 0), (0, 0), (0, half - local)))
    last = jnp.concatenate([last, last], -1)
    psf = psf_spectrum.reshape(2 * depth * local, columns)
    estimate = lax.dynamic_slice_in_dim(estimate, lax.axis_index("view") * share, share, 0)
    levels = max(views.bit_length() - 1, 1)
    big = pltpu.VMEM((space * views * block, columns), jnp.float32)
    small = pltpu.VMEM((space * block, columns), jnp.float32)
    operands = (observed[0], valid[0], psf, last) + tables
    call = pl.pallas_call(
        functools.partial(iterations_kernel, (space, views, planes, share, rows, columns, depth)),
        out_shape=jax.ShapeDtypeStruct((planes, rows, columns), jnp.float32),
        in_specs=[pl.BlockSpec(memory_space=pltpu.VMEM)] * (len(operands) + 1),
        out_specs=pl.BlockSpec(memory_space=pltpu.VMEM),
        scratch_shapes=[
            pltpu.VMEM(estimate.shape, jnp.float32),
            small, big, big, big, big, big, big,
            pltpu.VMEM((levels * views * space * block, columns), jnp.float32),
            small, small,
            pltpu.SemaphoreType.DMA((2, space)),
            pltpu.SemaphoreType.DMA((2, levels, space, views)),
            pltpu.SemaphoreType.DMA((2, views, space)),
            pltpu.SemaphoreType.DMA((2, views, space)),
            pltpu.SemaphoreType.DMA((2, levels, views, space)),
            pltpu.SemaphoreType.DMA((2, space)),
            pltpu.SemaphoreType.DMA((2, levels, views)),
        ],
        compiler_params=pltpu.CompilerParams(
            collective_id=0, has_side_effects=True, vmem_limit_bytes=56 * 1024 * 1024
        ),
        name="iterations",
    )
    return call(estimate, *operands)


def fits(mesh, estimate, observed):
    space, views = mesh.shape["space"], mesh.shape["view"]
    planes = estimate.shape[0] // space
    local = observed.shape[2] // mesh.shape["blocks"] // space
    return (
        planes % views == 0
        and planes // views <= 8
        and local % 8 == 0
        and views > 1
        and views & (views - 1) == 0
        and observed.shape[0] == views
    )


def solution(mesh):
    def mapped(body):
        return jax.shard_map(
            body,
            mesh=mesh,
            in_specs=(
                P("space", "blocks", None),
                P("view", "space", "blocks", None),
                P("view", "space", "blocks", None),
                P("view", None, None, "space", None),
            ),
            out_specs=P("space", "blocks", None),
            check_vma=False,
        )

    def refine(estimate, observed, valid, psf_spectrum):
        body = kernel_shards if fits(mesh, estimate, observed) else shards
        return mapped(body)(estimate, observed, valid, psf_spectrum)

    return refine
```
